32 devices in a mesh: ctx: 8 (over z, x), head: 4 (over y, core).
Axes of the slice: x: 2, y: 2, z: 4, core: 2. Of those that a mesh axis runs over, the one named last changes fastest.
Arguments:
- events: bfloat16 [6144, 1024], P('ctx', 'head'), may hold values from -3 to 3
- norm_gain: float32 [1024], replicated, may hold values from 0.5 to 1.5
- w_uvqk: bfloat16 [1024, 4, 1024], P(None, None, 'head'), may hold values from -4 to 4
- w_out: bfloat16 [1024, 1024], P('head'), may hold values from -0.1875 to 0.1875
- lengths: int32 [8], replicated, may hold values from 1 to 4608, 6144 in all
Outputs:
- mixed: bfloat16 [6144, 1024], P('ctx', 'head')
The draws below stay inside these ranges and needn't reach their ends.
Inputs may be any that keep to these rules, and one draw needn't show every extreme that they name: The lengths sum to 6144; the longest is exactly 4608.
All inputs are finite; a program needn't handle non-finite values.
Results may differ from the reference program's by a relative error of at most 0.0062.
Values may be sent and summed in bfloat16 or wider, within the bound.
A program may use at most 128 MiB of HBM per device.

```python
import math
import jax
import jax.numpy as jnp
import numpy as np
from jax import lax

D = 1024
HEADS = 8
HDIM = 128
TOK_DEV = 768
SEQS = 8
TOKENS = 6144
LMAX = 4608


def pattern_prototype():
    hidden_entry = jnp.arange(D, dtype=jnp.int32)
    pattern_array = hidden_entry % 8 == 0
    polarity_entries = jnp.where(hidden_entry % 16 == 0, 1.0, -1.0).astype(jnp.float32)
    return (pattern_array, polarity_entries)


def draw_events(key, part):
    jitter_key, amp_key, period_key, shift_key = jax.random.split(key, 4)
    jitter = jax.random.truncated_normal(jitter_key, -3.0, 3.0, (TOKENS, D), jnp.float32)
    amplitude = jax.random.uniform(amp_key, (4, D), jnp.float32, 0.4, 1.0)
    period = TOK_DEV * jnp.exp(jax.random.uniform(period_key, (4, D), jnp.float32, math.log(1.5), math.log(12.0)))
    phase_shift = jax.random.uniform(shift_key, (4, D), jnp.float32, -math.pi, math.pi)
    position = jnp.arange(TOKENS, dtype=jnp.float32)
    smooth = jnp.zeros((TOKENS, D), jnp.float32)
    for term_index in range(4):
        angle_rate = 2.0 * math.pi / period[term_index]
        smooth = smooth + amplitude[term_index][None, :] * jnp.sin(position[:, None] * angle_rate[None, :] + phase_shift[term_index][None, :])
    pattern_array, polarity_entries = pattern_prototype()
    baseline_strength = jnp.where(pattern_array, 0.8 * polarity_entries, 0.0).astype(jnp.float32)
    return (0.25 * (jitter + smooth) + baseline_strength[None, :]).astype(jnp.bfloat16)


def draw_w_uvqk(key, part):
    base_key, spread_key = jax.random.split(key)
    factor = D ** (-0.5)
    base = jax.random.truncated_normal(base_key, -4.0, 4.0, (D, 4, D), jnp.float32)
    spread = jax.random.uniform(spread_key, (D, 4, D), jnp.float32, 0.5, 1.5)
    pattern_array, polarity_entries = pattern_prototype()
    column_scale = jnp.array([1.0, 2.0, 6.0, 4.0], jnp.float32)
    displacement_size = jnp.array([0.0, -0.64, 0.0, -2.26], jnp.float32)
    noise_part = factor * column_scale[None, :, None] * base
    modulated_entries = 8.0 / D * polarity_entries[:, None, None] * displacement_size[None, :, None] * spread
    modulate_input = pattern_array[:, None, None] & (displacement_size != 0.0)[None, :, None]
    return jnp.where(modulate_input, modulated_entries, noise_part).astype(jnp.bfloat16)


def shard_levels(rng, extent, shards, low, largest):
    def one(dim, parts):
        draws = jax.random.uniform(jax.random.fold_in(jax.random.fold_in(rng, 6), dim), (parts,), jnp.float32, low / len(shards), largest / len(shards))
        return jnp.repeat(jnp.exp(draws), extent[dim] // parts).reshape((-1,) + (1,) * (len(extent) - dim - 1))

    loudness = one(*shards[0])
    for cut in shards[1:]:
        loudness = loudness * one(*cut)
    return loudness


def profile(amount, total, reach, slope):
    loads = [(1 << 20) // math.isqrt(standing ** slope) + 1 for standing in range(2, amount + 1)]
    spare, given = total - reach - (amount - 1), [1] * (amount - 1)
    while spare > 0:
        candidates = [i for i in range(amount - 1) if given[i] < reach]
        mass, left = sum([loads[i] for i in candidates]), spare
        for i in candidates:
            extra = min(reach - given[i], max(1, left * loads[i] // mass), spare)
            given[i] = given[i] + extra
            spare = spare - extra
    return np.array([reach] + given)


def uneven_parts(stream_key, amount, total, bound, skew):
    if amount == 2:
        one = jax.random.randint(stream_key, (), max(1, total - bound), min(bound, total - 1) + 1)
        return jnp.stack([one, total - one])
    tallies = jnp.asarray(profile(amount, total, bound, skew), jnp.int32)
    couples = (amount - 1) // 2
    source_of, receiver = tallies[1:1 + 2 * couples:2], tallies[2:2 + 2 * couples:2]
    margin = jnp.minimum(source_of - 1, bound - receiver)
    moved = jax.random.randint(jax.random.fold_in(stream_key, 1), (couples,), 0, 1 << 20) % (margin + 1)
    tallies = tallies.at[1:1 + 2 * couples:2].set(source_of - moved).at[2:2 + 2 * couples:2].set(receiver + moved)
    return tallies[jax.random.permutation(jax.random.fold_in(stream_key, 2), amount)]


def noise(key, extent, scale, most, cuts=(), held_as=jnp.bfloat16):
    values = jax.random.normal(key, extent, jnp.float32) * scale
    if len(cuts) > 0:
        values = shard_levels(key, extent, cuts, -0.22, 0.18) * values
    return jnp.clip(values, min=-most, max=most).astype(held_as)


def setup_inputs(seed: int = 0) -> dict:
    keys = jax.random.split(jax.random.key(seed), 6)
    return {
        "events": draw_events(jax.random.fold_in(keys[5], 71), 0),
        "norm_gain": jnp.clip(1.0 + 0.1 * jax.random.normal(keys[1], (D,), jnp.float32), 0.5, 1.5),
        "w_uvqk": draw_w_uvqk(jax.random.fold_in(keys[5], 71), 0),
        "w_out": noise(keys[3], (D, D), D ** -0.5, 0.1875, ((0, 4),)),
        "lengths": uneven_parts(keys[4], SEQS, TOKENS, LMAX, 2).astype(jnp.int32),
    }


def reference(events, norm_gain, w_uvqk, w_out, lengths):
    epsilon = 1e-05
    xfloat = events.astype(jnp.float32)
    row_mean = lax.optimization_barrier(jnp.mean(xfloat, axis=-1, keepdims=True))
    centered = xfloat - row_mean
    row_var = lax.optimization_barrier(jnp.mean(centered * centered, axis=-1, keepdims=True))
    normed = (centered * lax.rsqrt(row_var + epsilon) * norm_gain).astype(jnp.bfloat16)
    projected = jax.nn.silu(jnp.dot(normed, w_uvqk.reshape(D, 4 * D), preferred_element_type=jnp.float32)).astype(jnp.bfloat16)
    projected = projected.reshape(TOKENS, 4, HEADS, HDIM)
    gate_rows = projected[:, 0]
    value_rows = projected[:, 1].astype(jnp.float32)
    query_rows = projected[:, 2].astype(jnp.float32)
    key_rows = projected[:, 3].astype(jnp.float32)
    seq_ends = jnp.cumsum(lengths).astype(jnp.int32)
    positions = jnp.arange(TOKENS, dtype=jnp.int32)
    segment = lax.optimization_barrier(jnp.sum((positions[:, None] >= seq_ends[None, :]).astype(jnp.int32), axis=1))
    score_scale = HDIM ** (-0.5)
    block_size = math.gcd(TOKENS, 256)
    block_count = TOKENS // block_size

    def one_block(block_index):
        first_row = (block_index * block_size).astype(jnp.int32)
        queries = lax.dynamic_slice_in_dim(query_rows, first_row, block_size, 0)
        query_pos = first_row + jnp.arange(block_size, dtype=jnp.int32)
        query_seg = lax.dynamic_slice_in_dim(segment, first_row, block_size, 0)
        scores = jnp.einsum('qhd,khd->hqk', queries, key_rows) * score_scale
        allowed = (query_seg[:, None] == segment[None, :]) & (positions[None, :] <= query_pos[:, None])
        weights = jnp.where(allowed[None], jax.nn.silu(scores), 0.0).astype(jnp.bfloat16)
        return jnp.einsum('hqk,khd->qhd', weights.astype(jnp.float32), value_rows)
    attended = lax.map(one_block, jnp.arange(block_count, dtype=jnp.int32)).reshape(TOKENS, HEADS, HDIM)
    squares = lax.optimization_barrier(jnp.sum(attended * attended, axis=(1, 2)))
    inverse_rms = lax.rsqrt(squares / D + epsilon)
    gated = (attended * inverse_rms[:, None, None] * gate_rows.astype(jnp.float32)).astype(jnp.bfloat16).reshape(TOKENS, D)
    mixed = xfloat + jnp.dot(gated, w_out, preferred_element_type=jnp.float32)
    return mixed.astype(jnp.bfloat16)
```

```python
import functools

import jax
import jax.numpy as jnp
from jax import lax
from jax.experimental import pallas as pl
from jax.experimental.pallas import tpu as pltpu
from jax.sharding import PartitionSpec as P

HDIM = 128
EPS = 1e-05
MESH = pl.DeviceIdType.MESH
F32 = jnp.float32
BF16 = jnp.bfloat16


def silu(z):
    t = 0.5 * z
    return t + t * jnp.tanh(t)


def kernel(
    line, ev, gain, w, wout, lengths, out,
    xall, nbuf, kbuf, vbuf, gate, qbuf, resf, res_in, res_out, att, gs, go, sqs, sqall, wall,
    sA, rA, qs, qr, rs, rr, sE, rE, ws, wr, ss, sr,
):
    T, F = ev.shape
    D = xall.shape[1]
    C = T // 2
    SLAB = 2 * T
    NC = 4
    KT = 256 if SLAB % 256 == 0 else C
    c = lax.axis_index("ctx")
    h = lax.axis_index("head")
    x = c % 2
    ox = 1 - x
    zz = c // 2
    sh = h + 1 - 2 * (h % 2)
    yh = (h + 2) % 4
    me = (c, h)
    sib = (c, sh)
    yn = (c, yh)
    xc = c + 1 - 2 * x
    xn = (xc, h)
    prv = (c - 2, h)
    nxt = (c + 2, h)
    hasp = zz > 0
    hasn = zz < line - 1
    peers = [(c if dx == 0 else xc, (h + dh) % 4, dx, dh) for dx in (0, 1) for dh in range(4) if dx + dh > 0]

    def rc(src, dst, ssem, rsem, dev):
        return pltpu.make_async_remote_copy(
            src_ref=src, dst_ref=dst, send_sem=ssem, recv_sem=rsem, device_id=dev, device_id_type=MESH
        )

    bar = pltpu.get_barrier_semaphore()
    for pc, ph, _, _ in peers:
        pl.semaphore_signal(bar, inc=1, device_id=(pc, ph), device_id_type=MESH)

    @pl.when(hasp)
    def _():
        pl.semaphore_signal(bar, inc=1, device_id=prv, device_id_type=MESH)

    @pl.when(hasn)
    def _():
        pl.semaphore_signal(bar, inc=1, device_id=nxt, device_id_type=MESH)

    pl.semaphore_wait(bar, 7 + hasp.astype(jnp.int32) + hasn.astype(jnp.int32))

    def al(v, m):
        return pl.multiple_of(v, m)

    def piece(g, r, hh):
        return xall.at[pl.ds(al(g * T + r * C, C), C), pl.ds(al(hh * F, F), F)]

    def own_copy(r, slot, kind, dev):
        return rc(ev.at[pl.ds(r * C, C)], piece(x, r, h), sA.at[slot, r], rA.at[kind, r], dev)

    def relay(g, r, hh, slot, kind, dev):
        p = piece(g, r, hh)
        return rc(p, p, sA.at[slot, r], rA.at[kind, r], dev)

    def got(g, r, hh, kind):
        p = piece(g, r, hh)
        rc(p, p, sA.at[0, r], rA.at[kind, r], sib).wait_recv()

    sendsA = []

    def go_send(d):
        d.start()
        sendsA.append(d)

    for r in (0, 1):
        go_send(own_copy(r, 1, 4, yn))
        go_send(own_copy(r, 2, 5, xn))
        go_send(own_copy(r, 0, 0, sib))
    xall[pl.ds(al(x * T, T), T), pl.ds(al(h * F, F), F)] = ev[...]

    def chunk_base(i):
        r = i % 2
        g = jnp.where(i < 2, x, ox)
        return al(g * T + r * C, C)

    LN = 64 if C % 64 == 0 else C

    def qcopy(s, i, dev):
        rows = pl.ds(chunk_base(i), C)
        return rc(qbuf.at[s, rows], qbuf.at[s, rows], qs.at[s, i], qr.at[s, i], dev)

    def project(i):
        base = chunk_base(i)

        def ln(k, carry):
            rows = pl.ds(al(base + k * LN, LN), LN)
            xf = xall[rows, :].astype(F32)
            mean = jnp.mean(xf, axis=-1, keepdims=True)
            cen = xf - mean
            var = jnp.mean(cen * cen, axis=-1, keepdims=True)
            nbuf[pl.ds(al(k * LN, LN), LN), :] = (cen * lax.rsqrt(var + EPS) * gain[...]).astype(BF16)
            return carry

        lax.fori_loop(0, C // LN, ln, 0)
        rows = pl.ds(base, C)
        for half in (1, 0):
            p = silu(
                jnp.dot(nbuf[...], w[:, half * 2 * HDIM:(half + 1) * 2 * HDIM], preferred_element_type=F32)
            ).astype(BF16)
            if half == 1:
                qbuf[zz, rows, :] = p[:, :HDIM]
                kbuf[rows, :] = p[:, HDIM:]

                @pl.when(hasp)
                def _():
                    qcopy(zz, i, prv).start()
            else:
                gate[rows, :] = p[:, :HDIM]
                vbuf[rows, :] = p[:, HDIM:]

    h3 = sh + 2 - 4 * (sh // 2)
    got(x, 0, yh, 4)
    go_send(relay(x, 0, yh, 3, 1, sib))
    got(ox, 0, h, 5)
    go_send(relay(ox, 0, h, 6, 6, yn))
    go_send(relay(ox, 0, h, 4, 2, sib))
    got(x, 0, sh, 0)
    got(x, 0, h3, 1)
    project(0)
    got(x, 1, yh, 4)
    go_send(relay(x, 1, yh, 6, 6, xn))
    go_send(relay(x, 1, yh, 3, 1, sib))
    got(ox, 1, h, 5)
    go_send(relay(ox, 1, h, 4, 2, sib))
    got(x, 1, sh, 0)
    got(x, 1, h3, 1)
    project(1)
    for r in (0, 1):
        got(ox, r, yh, 6)
        go_send(relay(ox, r, yh, 5, 3, sib))
    for dh in (1, 2, 3):
        ph = (h + dh) % 4
        go_send(
            rc(wout.at[:, pl.ds(al(ph * F, F), F)], wall.at[pl.ds(al(h * F, F), F)],
               ws.at[dh - 1], wr.at[dh - 1], (c, ph))
        )
    wall[pl.ds(al(h * F, F), F), :] = wout[:, pl.ds(al(h * F, F), F)]
    for r in (0, 1):
        got(ox, r, sh, 2)
        got(ox, r, h3, 3)
        project(2 + r)

    half_scale = 0.5 * HDIM ** (-0.5)

    def starts_of(first):
        pos = first + lax.broadcasted_iota(jnp.int32, (C, 1), 0)
        end = jnp.int32(0)
        start = jnp.zeros((C, 1), jnp.int32)
        for s in range(lengths.shape[0]):
            end = end + lengths[s]
            start = jnp.where(pos >= end, end, start)
        return pos, start

    def tile_sum(q, start, pos, k0):
        rows = pl.ds(k0, KT)
        t = lax.dot_general(q, kbuf[rows, :], (((1,), (1,)), ((), ())), preferred_element_type=F32) * half_scale
        wgt = t + t * jnp.tanh(t)
        kpos = zz * SLAB + k0 + lax.broadcasted_iota(jnp.int32, (1, KT), 1)
        allowed = kpos >= start
        if pos is not None:
            allowed = allowed & (kpos <= pos)
        wgt = jnp.where(allowed, wgt, 0.0).astype(BF16)
        return jnp.dot(wgt, vbuf[rows, :], preferred_element_type=F32)

    def rcopy(s, i, dev):
        rows = pl.ds(chunk_base(i), C)
        return rc(res_out.at[s, rows], res_in.at[s, rows], rs.at[s, i], rr.at[s, i], dev)

    def incoming(t, carry):
        s = zz + 1 + t // NC
        i = t % NC
        base = chunk_base(i)
        qcopy(s, i, prv).wait_recv()

        @pl.when(hasp)
        def _():
            qcopy(s, i, prv).start()

        rows = pl.ds(base, C)
        q = qbuf[s, rows, :]
        _, start = starts_of(s * SLAB + base)
        total = jnp.zeros((C, HDIM), F32)
        for k in range(SLAB // KT):
            total = total + tile_sum(q, start, None, k * KT)

        @pl.when(hasp)
        def _():
            resf[s, rows, :] = total

        @pl.when(zz == 0)
        def _():
            res_out[s, rows, :] = total.astype(BF16)
            rcopy(s, i, nxt).start()

        return carry

    items = NC * (line - 1 - zz)
    lax.fori_loop(0, items, incoming, 0)

    def diagonal(i, carry):
        base = chunk_base(i)
        rows = pl.ds(base, C)
        q = qbuf[zz, rows, :]
        pos, start = starts_of(zz * SLAB + base)
        att[rows, :] = jnp.zeros((C, HDIM), F32)

        def one(k, carry):
            att[rows, :] += tile_sum(q, start, pos, al(k * KT, KT))
            return carry

        lax.fori_loop(0, (base + C + KT - 1) // KT, one, 0)
        return carry

    lax.fori_loop(0, NC, diagonal, 0)

    @pl.when(hasp)
    def _():
        def onward(t, carry):
            s = zz + 1 + t // NC
            i = t % NC
            rows = pl.ds(chunk_base(i), C)
            rcopy(s, i, nxt).wait_recv()
            res_out[s, rows, :] = (resf[s, rows, :] + res_in[s, rows, :].astype(F32)).astype(BF16)
            rcopy(s, i, nxt).start()
            return carry

        lax.fori_loop(0, items, onward, 0)

    def epiece(xs, r, hs):
        return go.at[pl.ds(r * C, C), pl.ds(al(hs * F + xs * HDIM, HDIM), HDIM)]

    def erelay(xs, r, hs, slot, kind, dev):
        p = epiece(xs, r, hs)
        return rc(p, p, sE.at[slot, r], rE.at[kind, r], dev)

    def egot(xs, r, hs, kind):
        p = epiece(xs, r, hs)
        rc(p, p, sE.at[0, r], rE.at[kind, r], sib).wait_recv()

    ones = jnp.ones((8, HDIM), BF16)
    for i in range(NC):
        r = i % 2
        base = chunk_base(jnp.int32(i))
        rows = pl.ds(base, C)

        @pl.when(hasp)
        def _():
            rcopy(zz, i, nxt).wait_recv()
            att[rows, :] += res_in[zz, rows, :].astype(F32)

        a = att[rows, :]
        gs[rows, :] = (a * gate[rows, :].astype(F32)).astype(BF16)
        src = gs.at[rows]
        if i < 2:
            go_send(rc(src, epiece(x, r, h), sE.at[1, r], rE.at[4, r], yn))
            go_send(rc(src, epiece(x, r, h), sE.at[0, r], rE.at[0, r], sib))
            go[r * C:(r + 1) * C, pl.ds(al(h * F + x * HDIM, HDIM), HDIM)] = gs[rows, :]
        else:
            go_send(rc(src, epiece(x, r, h), sE.at[2, r], rE.at[5, r], xn))
        sq = a * a
        hi = sq.astype(BF16)
        lo = (sq - hi.astype(F32)).astype(BF16)
        dims = (((1,), (1,)), ((), ()))
        sqs[:, pl.ds(base, C)] = lax.dot_general(ones, hi, dims, preferred_element_type=F32) + lax.dot_general(
            ones, lo, dims, preferred_element_type=F32
        )
    for n, (pc, ph, dx, dh) in enumerate(peers):
        grp = x if dx == 0 else ox
        go_send(rc(sqs.at[:, pl.ds(al(grp * T, T), T)], sqall.at[n], ss.at[n], sr.at[n], (pc, ph)))
    for r in (0, 1):
        egot(x, r, yh, 4)
        go_send(erelay(x, r, yh, 3, 1, sib))
    for r in (0, 1):
        egot(ox, r, h, 5)
        go_send(erelay(ox, r, h, 6, 6, yn))
        go_send(erelay(ox, r, h, 4, 2, sib))
    for dh in (1, 2, 3):
        src_h = (h + 4 - dh) % 4
        rc(wout.at[:, pl.ds(0, F)], wall.at[pl.ds(al(src_h * F, F), F)], ws.at[dh - 1], wr.at[dh - 1], sib).wait_recv()
    squares = sqs[:, pl.ds(al(x * T, T), T)]
    for n in range(7):
        rc(sqs.at[:, pl.ds(0, T)], sqall.at[n], ss.at[n], sr.at[n], sib).wait_recv()
        squares = squares + sqall[n]
    inv = lax.rsqrt(squares / D + EPS)
    inv = jnp.broadcast_to(inv[0:1], (HDIM, T)).T
    for r in (0, 1):
        egot(ox, r, yh, 6)
        go_send(erelay(ox, r, yh, 5, 3, sib))
    for r in (0, 1):
        egot(x, r, sh, 0)
        egot(x, r, h3, 1)
        egot(ox, r, sh, 2)
        egot(ox, r, h3, 3)
        rows = slice(r * C, (r + 1) * C)
        prod = jnp.dot(go[rows, :], wall[...], preferred_element_type=F32)
        scale = inv[rows, :]
        for k in range(F // HDIM):
            cols = slice(k * HDIM, (k + 1) * HDIM)
            out[rows, cols] = (ev[rows, cols].astype(F32) + prod[:, cols] * scale).astype(BF16)

    for d in sendsA:
        d.wait_send()

    @pl.when(hasp)
    def _():
        def fin(t, carry):
            qcopy(zz + t // NC, t % NC, prv).wait_send()
            return carry

        lax.fori_loop(0, items + NC, fin, 0)

    def fin2(t, carry):
        rcopy(zz + 1 + t // NC, t % NC, nxt).wait_send()
        return carry

    lax.fori_loop(0, items, fin2, 0)


def shards(events, norm_gain, w_uvqk, w_out, lengths):
    T, F = events.shape
    D = w_uvqk.shape[0]
    line = lax.axis_size("ctx") // 2
    x = lax.axis_index("ctx") % 2
    w = lax.dynamic_slice_in_dim(w_uvqk, x * HDIM, HDIM, 2).reshape(D, 4 * HDIM)
    S = 2 * T
    vm = pltpu.VMEM
    dma = pltpu.SemaphoreType.DMA
    vspec = pl.BlockSpec(memory_space=pltpu.VMEM)
    return pl.pallas_call(
        functools.partial(kernel, line),
        out_shape=jax.ShapeDtypeStruct((T, F), BF16),
        in_specs=[vspec] * 4 + [pl.BlockSpec(memory_space=pltpu.SMEM)],
        out_specs=vspec,
        scratch_shapes=[
            vm((S, D), BF16), vm((T // 2, D), BF16), vm((S, HDIM), BF16), vm((S, HDIM), BF16), vm((S, HDIM), BF16),
            vm((line, S, HDIM), BF16), vm((line, S, HDIM), F32), vm((line, S, HDIM), BF16),
            vm((line, S, HDIM), BF16), vm((S, HDIM), F32), vm((S, HDIM), BF16), vm((T, D), BF16),
            vm((8, S), F32), vm((7, 8, T), F32), vm((D, F), BF16),
            dma((7, 2)), dma((7, 2)), dma((line, 4)), dma((line, 4)), dma((line, 4)), dma((line, 4)),
            dma((7, 2)), dma((7, 2)), dma((3,)), dma((3,)), dma((7,)), dma((7,)),
        ],
        compiler_params=pltpu.CompilerParams(
            collective_id=0, has_side_effects=True, vmem_limit_bytes=56 * 1024 * 1024
        ),
    )(events, norm_gain.reshape(1, D), w, w_out, lengths)


def solution(mesh):
    in_specs = (P("ctx", "head"), P(), P(None, None, "head"), P("head", None), P())
    return jax.shard_map(shards, mesh=mesh, in_specs=in_specs, out_specs=P("ctx", "head"), check_vma=False)
```

```python
import functools

import jax
import jax.numpy as jnp
from jax import lax
from jax.experimental import pallas as pl
from jax.experimental.pallas import tpu as pltpu
from jax.sharding import PartitionSpec as P

HDIM = 128
EPS = 1e-05
MESH = pl.DeviceIdType.MESH
F32 = jnp.float32
BF16 = jnp.bfloat16


def silu(z):
    t = 0.5 * z
    return t + t * jnp.tanh(t)


def kernel(
    line, ev, gain, w, wout, lengths, out,
    xall, nbuf, kbuf, wgt_buf, vbuf, gate, qbuf, resf, res_in, res_out, att, gs, go, sqs, sqall, wall,
    sA, rA, qs, qr, rs, rr, sE, rE, ws, wr, ss, sr,
):
    T, F = ev.shape
    D = xall.shape[1]
    C = T // 2
    SLAB = 2 * T
    NC = 4
    KT = 256 if SLAB % 256 == 0 else C
    c = lax.axis_index("ctx")
    h = lax.axis_index("head")
    x = c % 2
    ox = 1 - x
    zz = c // 2
    sh = h + 1 - 2 * (h % 2)
    yh = (h + 2) % 4
    me = (c, h)
    sib = (c, sh)
    yn = (c, yh)
    xc = c + 1 - 2 * x
    xn = (xc, h)
    prv = (c - 2, h)
    nxt = (c + 2, h)
    hasp = zz > 0
    hasn = zz < line - 1
    peers = [(c if dx == 0 else xc, (h + dh) % 4, dx, dh) for dx in (0, 1) for dh in range(4) if dx + dh > 0]

    def rc(src, dst, ssem, rsem, dev):
        return pltpu.make_async_remote_copy(
            src_ref=src, dst_ref=dst, send_sem=ssem, recv_sem=rsem, device_id=dev, device_id_type=MESH
        )

    bar = pltpu.get_barrier_semaphore()
    for pc, ph, _, _ in peers:
        pl.semaphore_signal(bar, inc=1, device_id=(pc, ph), device_id_type=MESH)

    @pl.when(hasp)
    def _():
        pl.semaphore_signal(bar, inc=1, device_id=prv, device_id_type=MESH)

    @pl.when(hasn)
    def _():
        pl.semaphore_signal(bar, inc=1, device_id=nxt, device_id_type=MESH)

    pl.semaphore_wait(bar, 7 + hasp.astype(jnp.int32) + hasn.astype(jnp.int32))

    def al(v, m):
        return pl.multiple_of(v, m)

    def piece(g, r, hh):
        return xall.at[pl.ds(al(g * T + r * C, C), C), pl.ds(al(hh * F, F), F)]

    def own_copy(r, slot, kind, dev):
        return rc(ev.at[pl.ds(r * C, C)], piece(x, r, h), sA.at[slot, r], rA.at[kind, r], dev)

    def relay(g, r, hh, slot, kind, dev):
        p = piece(g, r, hh)
        return rc(p, p, sA.at[slot, r], rA.at[kind, r], dev)

    def got(g, r, hh, kind):
        p = piece(g, r, hh)
        rc(p, p, sA.at[0, r], rA.at[kind, r], sib).wait_recv()

    sendsA = []

    def go_send(d):
        d.start()
        sendsA.append(d)

    for r in (0, 1):
        go_send(own_copy(r, 1, 4, yn))
        go_send(own_copy(r, 2, 5, xn))
        go_send(own_copy(r, 0, 0, sib))
    xall[pl.ds(al(x * T, T), T), pl.ds(al(h * F, F), F)] = ev[...]

    def chunk_base(i):
        r = i % 2
        g = jnp.where(i < 2, x, ox)
        return al(g * T + r * C, C)

    RB = 128 if C % 128 == 0 else C
    LN = 64 if C % 64 == 0 else C

    def qcopy(s, i, dev):
        rows = pl.ds(chunk_base(i), C)
        return rc(qbuf.at[s, rows], qbuf.at[s, rows], qs.at[s, i], qr.at[s, i], dev)

    def project(i):
        base = chunk_base(i)

        def ln(k, carry):
            rows = pl.ds(al(base + k * LN, LN), LN)
            xf = xall[rows, :].astype(F32)
            mean = jnp.mean(xf, axis=-1, keepdims=True)
            cen = xf - mean
            var = jnp.mean(cen * cen, axis=-1, keepdims=True)
            nbuf[pl.ds(al(k * LN, LN), LN), :] = (cen * lax.rsqrt(var + EPS) * gain[...]).astype(BF16)
            return carry

        lax.fori_loop(0, C // LN, ln, 0)
        rows = pl.ds(base, C)
        for half in (1, 0):
            p = silu(
                jnp.dot(nbuf[...], w[:, half * 2 * HDIM:(half + 1) * 2 * HDIM], preferred_element_type=F32)
            ).astype(BF16)
            if half == 1:
                qbuf[zz, rows, :] = p[:, :HDIM]
                kbuf[:, rows] = p[:, HDIM:].astype(F32).T.astype(BF16)

                @pl.when(hasp)
                def _():
                    qcopy(zz, i, prv).start()
            else:
                gate[rows, :] = p[:, :HDIM]
                vbuf[rows, :] = p[:, HDIM:]

    h3 = sh + 2 - 4 * (sh // 2)
    got(x, 0, yh, 4)
    go_send(relay(x, 0, yh, 3, 1, sib))
    got(ox, 0, h, 5)
    go_send(relay(ox, 0, h, 6, 6, yn))
    go_send(relay(ox, 0, h, 4, 2, sib))
    got(x, 0, sh, 0)
    got(x, 0, h3, 1)
    project(0)
    got(x, 1, yh, 4)
    go_send(relay(x, 1, yh, 6, 6, xn))
    go_send(relay(x, 1, yh, 3, 1, sib))
    got(ox, 1, h, 5)
    go_send(relay(ox, 1, h, 4, 2, sib))
    got(x, 1, sh, 0)
    got(x, 1, h3, 1)
    project(1)
    for r in (0, 1):
        got(ox, r, yh, 6)
        go_send(relay(ox, r, yh, 5, 3, sib))
    for dh in (1, 2, 3):
        ph = (h + dh) % 4
        go_send(
            rc(wout.at[:, pl.ds(al(ph * F, F), F)], wall.at[pl.ds(al(h * F, F), F)],
               ws.at[dh - 1], wr.at[dh - 1], (c, ph))
        )
    wall[pl.ds(al(h * F, F), F), :] = wout[:, pl.ds(al(h * F, F), F)]
    for r in (0, 1):
        got(ox, r, sh, 2)
        got(ox, r, h3, 3)
        project(2 + r)

    half_scale = 0.5 * HDIM ** (-0.5)

    def starts_of(first):
        pos = first + lax.broadcasted_iota(jnp.int32, (C, 1), 0)
        end = jnp.int32(0)
        start = jnp.zeros((C, 1), jnp.int32)
        for s in range(lengths.shape[0]):
            end = end + lengths[s]
            start = jnp.where(pos >= end, end, start)
        return pos, start

    def tile_weights(q, start, pos, k0):
        t = jnp.dot(q, kbuf[:, pl.ds(k0, KT)], preferred_element_type=F32) * half_scale
        wgt = t + t * jnp.tanh(t)
        kpos = zz * SLAB + k0 + lax.broadcasted_iota(jnp.int32, (1, KT), 1)
        allowed = kpos >= start
        if pos is not None:
            allowed = allowed & (kpos <= pos)
        return jnp.where(allowed, wgt, 0.0).astype(BF16)

    def tile_sum(q, start, pos, k0):
        return jnp.dot(tile_weights(q, start, pos, k0), vbuf[pl.ds(k0, KT), :], preferred_element_type=F32)

    def rcopy(s, i, dev):
        rows = pl.ds(chunk_base(i), C)
        return rc(res_out.at[s, rows], res_in.at[s, rows], rs.at[s, i], rr.at[s, i], dev)

    def incoming(t, carry):
        s = zz + 1 + t // NC
        i = t % NC
        base = chunk_base(i)
        qcopy(s, i, prv).wait_recv()

        @pl.when(hasp)
        def _():
            qcopy(s, i, prv).start()

        rows = pl.ds(base, C)
        q = qbuf[s, rows, :]
        _, start = starts_of(s * SLAB + base)
        parts = []
        for b in range(C // RB):
            blk = slice(b * RB, (b + 1) * RB)
            for k in range(SLAB // KT):
                wgt_buf[blk, k * KT:(k + 1) * KT] = tile_weights(q[blk], start[blk], None, k * KT)
            parts.append(jnp.dot(wgt_buf[blk, :], vbuf[...], preferred_element_type=F32))
        total = jnp.concatenate(parts, axis=0)

        @pl.when(hasp)
        def _():
            resf[s, rows, :] = total

        @pl.when(zz == 0)
        def _():
            res_out[s, rows, :] = total.astype(BF16)
            rcopy(s, i, nxt).start()

        return carry

    items = NC * (line - 1 - zz)
    lax.fori_loop(0, items, incoming, 0)

    def diagonal(i, carry):
        base = chunk_base(i)
        rows = pl.ds(base, C)
        q = qbuf[zz, rows, :]
        pos, start = starts_of(zz * SLAB + base)
        att[rows, :] = jnp.zeros((C, HDIM), F32)

        def one(k, carry):
            att[rows, :] += tile_sum(q, start, pos, al(k * KT, KT))
            return carry

        lax.fori_loop(0, (base + C + KT - 1) // KT, one, 0)
        return carry

    lax.fori_loop(0, NC, diagonal, 0)

    @pl.when(hasp)
    def _():
        def onward(t, carry):
            s = zz + 1 + t // NC
            i = t % NC
            rows = pl.ds(chunk_base(i), C)
            rcopy(s, i, nxt).wait_recv()
            res_out[s, rows, :] = (resf[s, rows, :] + res_in[s, rows, :].astype(F32)).astype(BF16)
            rcopy(s, i, nxt).start()
            return carry

        lax.fori_loop(0, items, onward, 0)

    def epiece(xs, r, hs):
        return go.at[pl.ds(r * C, C), pl.ds(al(hs * F + xs * HDIM, HDIM), HDIM)]

    def erelay(xs, r, hs, slot, kind, dev):
        p = epiece(xs, r, hs)
        return rc(p, p, sE.at[slot, r], rE.at[kind, r], dev)

    def egot(xs, r, hs, kind):
        p = epiece(xs, r, hs)
        rc(p, p, sE.at[0, r], rE.at[kind, r], sib).wait_recv()

    ones = jnp.ones((8, HDIM), BF16)
    for i in range(NC):
        r = i % 2
        base = chunk_base(jnp.int32(i))
        rows = pl.ds(base, C)

        @pl.when(hasp)
        def _():
            rcopy(zz, i, nxt).wait_recv()
            att[rows, :] += res_in[zz, rows, :].astype(F32)

        a = att[rows, :]
        gs[rows, :] = (a * gate[rows, :].astype(F32)).astype(BF16)
        src = gs.at[rows]
        if i < 2:
            go_send(rc(src, epiece(x, r, h), sE.at[1, r], rE.at[4, r], yn))
            go_send(rc(src, epiece(x, r, h), sE.at[0, r], rE.at[0, r], sib))
            go[r * C:(r + 1) * C, pl.ds(al(h * F + x * HDIM, HDIM), HDIM)] = gs[rows, :]
        else:
            go_send(rc(src, epiece(x, r, h), sE.at[2, r], rE.at[5, r], xn))
        sq = a * a
        hi = sq.astype(BF16)
        lo = (sq - hi.astype(F32)).astype(BF16)
        dims = (((1,), (1,)), ((), ()))
        sqs[:, pl.ds(base, C)] = lax.dot_general(ones, hi, dims, preferred_element_type=F32) + lax.dot_general(
            ones, lo, dims, preferred_element_type=F32
        )
    for n, (pc, ph, dx, dh) in enumerate(peers):
        grp = x if dx == 0 else ox
        go_send(rc(sqs.at[:, pl.ds(al(grp * T, T), T)], sqall.at[n], ss.at[n], sr.at[n], (pc, ph)))
    for r in (0, 1):
        egot(x, r, yh, 4)
        go_send(erelay(x, r, yh, 3, 1, sib))
    for r in (0, 1):
        egot(ox, r, h, 5)
        go_send(erelay(ox, r, h, 6, 6, yn))
        go_send(erelay(ox, r, h, 4, 2, sib))
    for dh in (1, 2, 3):
        src_h = (h + 4 - dh) % 4
        rc(wout.at[:, pl.ds(0, F)], wall.at[pl.ds(al(src_h * F, F), F)], ws.at[dh - 1], wr.at[dh - 1], sib).wait_recv()
    squares = sqs[:, pl.ds(al(x * T, T), T)]
    for n in range(7):
        rc(sqs.at[:, pl.ds(0, T)], sqall.at[n], ss.at[n], sr.at[n], sib).wait_recv()
        squares = squares + sqall[n]
    inv = lax.rsqrt(squares / D + EPS)
    inv = jnp.broadcast_to(inv[0:1], (HDIM, T)).T
    for r in (0, 1):
        egot(ox, r, yh, 6)
        go_send(erelay(ox, r, yh, 5, 3, sib))
    for r in (0, 1):
        egot(x, r, sh, 0)
        egot(x, r, h3, 1)
        egot(ox, r, sh, 2)
        egot(ox, r, h3, 3)
        rows = slice(r * C, (r + 1) * C)
        prod = jnp.dot(go[rows, :], wall[...], preferred_element_type=F32)
        scale = inv[rows, :]
        for k in range(F // HDIM):
            cols = slice(k * HDIM, (k + 1) * HDIM)
            out[rows, cols] = prod[:, cols] * scale

    for d in sendsA:
        d.wait_send()

    @pl.when(hasp)
    def _():
        def fin(t, carry):
            qcopy(zz + t // NC, t % NC, prv).wait_send()
            return carry

        lax.fori_loop(0, items + NC, fin, 0)

    def fin2(t, carry):
        rcopy(zz + 1 + t // NC, t % NC, nxt).wait_send()
        return carry

    lax.fori_loop(0, items, fin2, 0)


def shards(events, norm_gain, w_uvqk, w_out, lengths):
    T, F = events.shape
    D = w_uvqk.shape[0]
    line = lax.axis_size("ctx") // 2
    x = lax.axis_index("ctx") % 2
    w = lax.dynamic_slice_in_dim(w_uvqk, x * HDIM, HDIM, 2).reshape(D, 4 * HDIM)
    S = 2 * T
    vm = pltpu.VMEM
    dma = pltpu.SemaphoreType.DMA
    vspec = pl.BlockSpec(memory_space=pltpu.VMEM)
    delta = pl.pallas_call(
        functools.partial(kernel, line),
        out_shape=jax.ShapeDtypeStruct((T, F), F32),
        in_specs=[vspec] * 4 + [pl.BlockSpec(memory_space=pltpu.SMEM)],
        out_specs=vspec,
        scratch_shapes=[
            vm((S, D), BF16), vm((T // 2, D), BF16), vm((HDIM, S), BF16), vm((T // 2, S), BF16), vm((S, HDIM), BF16),
            vm((S, HDIM), BF16),
            vm((line, S, HDIM), BF16), vm((line, S, HDIM), F32), vm((line, S, HDIM), BF16),
            vm((line, S, HDIM), BF16), vm((S, HDIM), F32), vm((S, HDIM), BF16), vm((T, D), BF16),
            vm((8, S), F32), vm((7, 8, T), F32), vm((D, F), BF16),
            dma((7, 2)), dma((7, 2)), dma((line, 4)), dma((line, 4)), dma((line, 4)), dma((line, 4)),
            dma((7, 2)), dma((7, 2)), dma((3,)), dma((3,)), dma((7,)), dma((7,)),
        ],
        compiler_params=pltpu.CompilerParams(
            collective_id=0, has_side_effects=True, vmem_limit_bytes=56 * 1024 * 1024
        ),
    )(events, norm_gain.reshape(1, D), w, w_out, lengths)
    return (events.astype(F32) + delta).astype(BF16)


def solution(mesh):
    in_specs = (P("ctx", "head"), P(), P(None, None, "head"), P("head", None), P())
    return jax.shard_map(shards, mesh=mesh, in_specs=in_specs, out_specs=P("ctx", "head"), check_vma=False)
```

```python
import functools

import jax
import jax.numpy as jnp
from jax import lax
from jax.experimental import pallas as pl
from jax.experimental.pallas import tpu as pltpu
from jax.sharding import PartitionSpec as P

HDIM = 128
EPS = 1e-05
MESH = pl.DeviceIdType.MESH
F32 = jnp.float32
BF16 = jnp.bfloat16


def silu(z):
    t = 0.5 * z
    return t + t * jnp.tanh(t)


def kernel(
    line, ev, gain, w, wout, lengths, out,
    xall, nbuf, kbuf, wgt_buf, vbuf, kprev, vprev, gate, qbuf, resf, res_in, res_out, att, gs, go, sqs, sqall, wall,
    sA, rA, qs, qr, rs, rr, sE, rE, ws, wr, ss, sr, ks, kr, vs, vr,
):
    T, F = ev.shape
    D = xall.shape[1]
    C = T // 2
    SLAB = 2 * T
    NC = 4
    KT = 256 if SLAB % 256 == 0 else C
    c = lax.axis_index("ctx")
    h = lax.axis_index("head")
    x = c % 2
    ox = 1 - x
    zz = c // 2
    sh = h + 1 - 2 * (h % 2)
    yh = (h + 2) % 4
    me = (c, h)
    sib = (c, sh)
    yn = (c, yh)
    xc = c + 1 - 2 * x
    xn = (xc, h)
    prv = (c - 2, h)
    nxt = (c + 2, h)
    hasp = zz > 0
    hasn = zz < line - 1
    peers = [(c if dx == 0 else xc, (h + dh) % 4, dx, dh) for dx in (0, 1) for dh in range(4) if dx + dh > 0]

    def rc(src, dst, ssem, rsem, dev):
        return pltpu.make_async_remote_copy(
            src_ref=src, dst_ref=dst, send_sem=ssem, recv_sem=rsem, device_id=dev, device_id_type=MESH
        )

    bar = pltpu.get_barrier_semaphore()
    for pc, ph, _, _ in peers:
        pl.semaphore_signal(bar, inc=1, device_id=(pc, ph), device_id_type=MESH)

    @pl.when(hasp)
    def _():
        pl.semaphore_signal(bar, inc=1, device_id=prv, device_id_type=MESH)

    @pl.when(hasn)
    def _():
        pl.semaphore_signal(bar, inc=1, device_id=nxt, device_id_type=MESH)

    pl.semaphore_wait(bar, 7 + hasp.astype(jnp.int32) + hasn.astype(jnp.int32))

    def al(v, m):
        return pl.multiple_of(v, m)

    def piece(g, r, hh):
        return xall.at[pl.ds(al(g * T + r * C, C), C), pl.ds(al(hh * F, F), F)]

    def own_copy(r, slot, kind, dev):
        return rc(ev.at[pl.ds(r * C, C)], piece(x, r, h), sA.at[slot, r], rA.at[kind, r], dev)

    def relay(g, r, hh, slot, kind, dev):
        p = piece(g, r, hh)
        return rc(p, p, sA.at[slot, r], rA.at[kind, r], dev)

    def got(g, r, hh, kind):
        p = piece(g, r, hh)
        rc(p, p, sA.at[0, r], rA.at[kind, r], sib).wait_recv()

    sendsA = []

    def go_send(d):
        d.start()
        sendsA.append(d)

    for r in (0, 1):
        go_send(own_copy(r, 1, 4, yn))
        go_send(own_copy(r, 2, 5, xn))
        go_send(own_copy(r, 0, 0, sib))
    xall[pl.ds(al(x * T, T), T), pl.ds(al(h * F, F), F)] = ev[...]

    def chunk_base(i):
        r = i % 2
        g = jnp.where(i < 2, x, ox)
        return al(g * T + r * C, C)

    RB = 128 if C % 128 == 0 else C
    LN = 64 if C % 64 == 0 else C

    def qcopy(s, i, dev):
        rows = pl.ds(chunk_base(i), C)
        return rc(qbuf.at[s, rows], qbuf.at[s, rows], qs.at[s, i], qr.at[s, i], dev)

    def kcopy(i):
        cols = pl.ds(chunk_base(i), C)
        return rc(kbuf.at[:, cols], kprev.at[:, cols], ks.at[i], kr.at[i], nxt)

    def vcopy(i):
        rows = pl.ds(chunk_base(i), C)
        return rc(vbuf.at[rows], vprev.at[rows], vs.at[i], vr.at[i], nxt)

    def project(i):
        base = chunk_base(i)

        def ln(k, carry):
            rows = pl.ds(al(base + k * LN, LN), LN)
            xf = xall[rows, :].astype(F32)
            mean = jnp.mean(xf, axis=-1, keepdims=True)
            cen = xf - mean
            var = jnp.mean(cen * cen, axis=-1, keepdims=True)
            nbuf[pl.ds(al(k * LN, LN), LN), :] = (cen * lax.rsqrt(var + EPS) * gain[...]).astype(BF16)
            return carry

        lax.fori_loop(0, C // LN, ln, 0)
        rows = pl.ds(base, C)
        for half in (1, 0):
            p = silu(
                jnp.dot(nbuf[...], w[:, half * 2 * HDIM:(half + 1) * 2 * HDIM], preferred_element_type=F32)
            ).astype(BF16)
            if half == 1:
                qbuf[zz, rows, :] = p[:, :HDIM]
                kbuf[:, rows] = p[:, HDIM:].astype(F32).T.astype(BF16)

                @pl.when(zz > 1)
                def _():
                    qcopy(zz, i, prv).start()

                @pl.when(hasn)
                def _():
                    kcopy(i).start()
            else:
                gate[rows, :] = p[:, :HDIM]
                vbuf[rows, :] = p[:, HDIM:]

                @pl.when(hasn)
                def _():
                    vcopy(i).start()

    h3 = sh + 2 - 4 * (sh // 2)
    got(x, 0, yh, 4)
    go_send(relay(x, 0, yh, 3, 1, sib))
    got(ox, 0, h, 5)
    go_send(relay(ox, 0, h, 6, 6, yn))
    go_send(relay(ox, 0, h, 4, 2, sib))
    got(x, 0, sh, 0)
    got(x, 0, h3, 1)
    project(0)
    got(x, 1, yh, 4)
    go_send(relay(x, 1, yh, 6, 6, xn))
    go_send(relay(x, 1, yh, 3, 1, sib))
    got(ox, 1, h, 5)
    go_send(relay(ox, 1, h, 4, 2, sib))
    got(x, 1, sh, 0)
    got(x, 1, h3, 1)
    project(1)
    for r in (0, 1):
        got(ox, r, yh, 6)
        go_send(relay(ox, r, yh, 5, 3, sib))
    for dh in (1, 2, 3):
        ph = (h + dh) % 4
        go_send(
            rc(wout.at[:, pl.ds(al(ph * F, F), F)], wall.at[pl.ds(al(h * F, F), F)],
               ws.at[dh - 1], wr.at[dh - 1], (c, ph))
        )
    wall[pl.ds(al(h * F, F), F), :] = wout[:, pl.ds(al(h * F, F), F)]
    for r in (0, 1):
        got(ox, r, sh, 2)
        got(ox, r, h3, 3)
        project(2 + r)

    half_scale = 0.5 * HDIM ** (-0.5)

    def starts_of(first):
        pos = first + lax.broadcasted_iota(jnp.int32, (C, 1), 0)
        end = jnp.int32(0)
        start = jnp.zeros((C, 1), jnp.int32)
        for s in range(lengths.shape[0]):
            end = end + lengths[s]
            start = jnp.where(pos >= end, end, start)
        return pos, start

    def tile_weights(q, start, pos, k0, keys, first):
        t = jnp.dot(q, keys[:, pl.ds(k0, KT)], preferred_element_type=F32) * half_scale
        wgt = t + t * jnp.tanh(t)
        kpos = first + k0 + lax.broadcasted_iota(jnp.int32, (1, KT), 1)
        allowed = kpos >= start
        if pos is not None:
            allowed = allowed & (kpos <= pos)
        return jnp.where(allowed, wgt, 0.0).astype(BF16)

    def whole_slab(q, start, keys, values, first):
        parts = []
        for b in range(C // RB):
            blk = slice(b * RB, (b + 1) * RB)
            for k in range(SLAB // KT):
                wgt_buf[blk, k * KT:(k + 1) * KT] = tile_weights(q[blk], start[blk], None, k * KT, keys, first)
            parts.append(jnp.dot(wgt_buf[blk, :], values[...], preferred_element_type=F32))
        return jnp.concatenate(parts, axis=0)

    def diagonal(i, carry):
        base = chunk_base(i)
        rows = pl.ds(base, C)
        q = qbuf[zz, rows, :]
        pos, start = starts_of(zz * SLAB + base)
        att[rows, :] = jnp.zeros((C, HDIM), F32)

        def one(k, carry):
            k0 = al(k * KT, KT)
            wgt = tile_weights(q, start, pos, k0, kbuf, zz * SLAB)
            att[rows, :] += jnp.dot(wgt, vbuf[pl.ds(k0, KT), :], preferred_element_type=F32)
            return carry

        lax.fori_loop(0, (base + C + KT - 1) // KT, one, 0)
        return carry

    @pl.when(zz == 0)
    def _():
        lax.fori_loop(0, NC, diagonal, 0)

    def rcopy(s, i, dev):
        rows = pl.ds(chunk_base(i), C)
        return rc(res_out.at[s, rows], res_in.at[s, rows], rs.at[s, i], rr.at[s, i], dev)

    def passing(i, carry):
        qcopy(zz + 1, i, prv).wait_recv()
        qcopy(zz + 1, i, prv).start()
        return carry

    @pl.when(hasp & hasn)
    def _():
        lax.fori_loop(0, NC, passing, 0)

    def incoming(t, carry):
        s = zz + 2 + t // NC
        i = t % NC
        base = chunk_base(i)
        qcopy(s, i, prv).wait_recv()

        @pl.when(hasp)
        def _():
            qcopy(s, i, prv).start()

        rows = pl.ds(base, C)
        q = qbuf[s, rows, :]
        _, start = starts_of(s * SLAB + base)
        total = whole_slab(q, start, kbuf, vbuf, zz * SLAB)

        @pl.when(hasp)
        def _():
            resf[s, rows, :] = total

        @pl.when(zz == 0)
        def _():
            res_out[s, rows, :] = total.astype(BF16)
            rcopy(s, i, nxt).start()

        return carry

    items = jnp.where(zz < line - 2, NC * (line - 2 - zz), 0)
    lax.fori_loop(0, items, incoming, 0)

    @pl.when(hasp)
    def _():
        lax.fori_loop(0, NC, diagonal, 0)

        for i in range(NC):
            kcopy(i).wait_recv()
            vcopy(i).wait_recv()

        def crossing(i, carry):
            base = chunk_base(i)
            rows = pl.ds(base, C)
            _, start = starts_of(zz * SLAB + base)
            att[rows, :] += whole_slab(qbuf[zz, rows, :], start, kprev, vprev, (zz - 1) * SLAB)
            return carry

        lax.fori_loop(0, NC, crossing, 0)

    def pass_on(s, i):
        rows = pl.ds(chunk_base(i), C)
        return rc(res_in.at[s, rows], res_in.at[s, rows], rs.at[s, i], rr.at[s, i], nxt)

    @pl.when(hasp & hasn)
    def _():
        def straight(i, carry):
            rcopy(zz + 1, i, nxt).wait_recv()
            pass_on(zz + 1, i).start()
            return carry

        lax.fori_loop(0, NC, straight, 0)

        def onward(t, carry):
            s = zz + 2 + t // NC
            i = t % NC
            rows = pl.ds(chunk_base(i), C)
            rcopy(s, i, nxt).wait_recv()
            res_out[s, rows, :] = (resf[s, rows, :] + res_in[s, rows, :].astype(F32)).astype(BF16)
            rcopy(s, i, nxt).start()
            return carry

        lax.fori_loop(0, items, onward, 0)

    def epiece(xs, r, hs):
        return go.at[pl.ds(r * C, C), pl.ds(al(hs * F + xs * HDIM, HDIM), HDIM)]

    def erelay(xs, r, hs, slot, kind, dev):
        p = epiece(xs, r, hs)
        return rc(p, p, sE.at[slot, r], rE.at[kind, r], dev)

    def egot(xs, r, hs, kind):
        p = epiece(xs, r, hs)
        rc(p, p, sE.at[0, r], rE.at[kind, r], sib).wait_recv()

    ones = jnp.ones((8, HDIM), BF16)
    for i in range(NC):
        r = i % 2
        base = chunk_base(jnp.int32(i))
        rows = pl.ds(base, C)

        @pl.when(zz > 1)
        def _():
            rcopy(zz, i, nxt).wait_recv()
            att[rows, :] += res_in[zz, rows, :].astype(F32)

        a = att[rows, :]
        gs[rows, :] = (a * gate[rows, :].astype(F32)).astype(BF16)
        src = gs.at[rows]
        if i < 2:
            go_send(rc(src, epiece(x, r, h), sE.at[1, r], rE.at[4, r], yn))
            go_send(rc(src, epiece(x, r, h), sE.at[0, r], rE.at[0, r], sib))
            go[r * C:(r + 1) * C, pl.ds(al(h * F + x * HDIM, HDIM), HDIM)] = gs[rows, :]
        else:
            go_send(rc(src, epiece(x, r, h), sE.at[2, r], rE.at[5, r], xn))
        sq = a * a
        hi = sq.astype(BF16)
        lo = (sq - hi.astype(F32)).astype(BF16)
        dims = (((1,), (1,)), ((), ()))
        sqs[:, pl.ds(base, C)] = lax.dot_general(ones, hi, dims, preferred_element_type=F32) + lax.dot_general(
            ones, lo, dims, preferred_element_type=F32
        )
    for n, (pc, ph, dx, dh) in enumerate(peers):
        grp = x if dx == 0 else ox
        go_send(rc(sqs.at[:, pl.ds(al(grp * T, T), T)], sqall.at[n], ss.at[n], sr.at[n], (pc, ph)))
    for r in (0, 1):
        egot(x, r, yh, 4)
        go_send(erelay(x, r, yh, 3, 1, sib))
    for r in (0, 1):
        egot(ox, r, h, 5)
        go_send(erelay(ox, r, h, 6, 6, yn))
        go_send(erelay(ox, r, h, 4, 2, sib))
    for dh in (1, 2, 3):
        src_h = (h + 4 - dh) % 4
        rc(wout.at[:, pl.ds(0, F)], wall.at[pl.ds(al(src_h * F, F), F)], ws.at[dh - 1], wr.at[dh - 1], sib).wait_recv()
    squares = sqs[:, pl.ds(al(x * T, T), T)]
    for n in range(7):
        rc(sqs.at[:, pl.ds(0, T)], sqall.at[n], ss.at[n], sr.at[n], sib).wait_recv()
        squares = squares + sqall[n]
    inv = lax.rsqrt(squares / D + EPS)
    inv = jnp.broadcast_to(inv[0:1], (HDIM, T)).T
    for r in (0, 1):
        egot(ox, r, yh, 6)
        go_send(erelay(ox, r, yh, 5, 3, sib))
    for r in (0, 1):
        egot(x, r, sh, 0)
        egot(x, r, h3, 1)
        egot(ox, r, sh, 2)
        egot(ox, r, h3, 3)
        rows = slice(r * C, (r + 1) * C)
        prod = jnp.dot(go[rows, :], wall[...], preferred_element_type=F32)
        scale = inv[rows, :]
        for k in range(F // HDIM):
            cols = slice(k * HDIM, (k + 1) * HDIM)
            out[rows, cols] = (ev[rows, cols].astype(F32) + prod[:, cols] * scale).astype(BF16)

    for d in sendsA:
        d.wait_send()

    @pl.when(hasn)
    def _():
        for i in range(NC):
            kcopy(i).wait_send()
            vcopy(i).wait_send()

    @pl.when(zz > 1)
    def _():
        for i in range(NC):
            qcopy(zz, i, prv).wait_send()

    @pl.when(hasp & hasn)
    def _():
        def fin(t, carry):
            qcopy(zz + 1 + t // NC, t % NC, prv).wait_send()
            rcopy(zz + 1 + t // NC, t % NC, nxt).wait_send()
            return carry

        lax.fori_loop(0, items + NC, fin, 0)

    @pl.when(zz == 0)
    def _():
        def fin(t, carry):
            rcopy(2 + t // NC, t % NC, nxt).wait_send()
            return carry

        lax.fori_loop(0, items, fin, 0)


def shards(events, norm_gain, w_uvqk, w_out, lengths):
    T, F = events.shape
    D = w_uvqk.shape[0]
    line = lax.axis_size("ctx") // 2
    x = lax.axis_index("ctx") % 2
    w = lax.dynamic_slice_in_dim(w_uvqk, x * HDIM, HDIM, 2).reshape(D, 4 * HDIM)
    S = 2 * T
    vm = pltpu.VMEM
    dma = pltpu.SemaphoreType.DMA
    vspec = pl.BlockSpec(memory_space=pltpu.VMEM)
    return pl.pallas_call(
        functools.partial(kernel, line),
        out_shape=jax.ShapeDtypeStruct((T, F), BF16),
        in_specs=[vspec] * 4 + [pl.BlockSpec(memory_space=pltpu.SMEM)],
        out_specs=vspec,
        scratch_shapes=[
            vm((S, D), BF16), vm((T // 2, D), BF16), vm((HDIM, S), BF16), vm((T // 2, S), BF16), vm((S, HDIM), BF16),
            vm((HDIM, S), BF16), vm((S, HDIM), BF16),
            vm((S, HDIM), BF16),
            vm((line, S, HDIM), BF16), vm((line, S, HDIM), F32), vm((line, S, HDIM), BF16),
            vm((line, S, HDIM), BF16), vm((S, HDIM), F32), vm((S, HDIM), BF16), vm((T, D), BF16),
            vm((8, S), F32), vm((7, 8, T), F32), vm((D, F), BF16),
            dma((7, 2)), dma((7, 2)), dma((line, 4)), dma((line, 4)), dma((line, 4)), dma((line, 4)),
            dma((7, 2)), dma((7, 2)), dma((3,)), dma((3,)), dma((7,)), dma((7,)),
            dma((4,)), dma((4,)), dma((4,)), dma((4,)),
        ],
        compiler_params=pltpu.CompilerParams(
            collective_id=0, has_side_effects=True, vmem_limit_bytes=56 * 1024 * 1024
        ),
    )(events, norm_gain.reshape(1, D), w, w_out, lengths)


def solution(mesh):
    in_specs = (P("ctx", "head"), P(), P(None, None, "head"), P("head", None), P())
    return jax.shard_map(shards, mesh=mesh, in_specs=in_specs, out_specs=P("ctx", "head"), check_vma=False)
```

```python
import functools

import jax
import jax.numpy as jnp
from jax import lax
from jax.experimental import pallas as pl
from jax.experimental.pallas import tpu as pltpu
from jax.sharding import PartitionSpec as P

HDIM = 128
EPS = 1e-05
MESH = pl.DeviceIdType.MESH
F32 = jnp.float32
BF16 = jnp.bfloat16


def silu(z):
    t = 0.5 * z
    return t + t * jnp.tanh(t)


def kernel(
    line, ev, gain, w, wout, lengths, out,
    xall, nbuf, kbuf, wgt_buf, vbuf, kprev, vprev, gate, qbuf, resf, res_in, res_out, att, gs, go, sqs, sqall, wall,
    sA, rA, qs, qr, rs, rr, sE, rE, ws, wr, ss, sr, ks, kr, vs, vr,
):
    T, F = ev.shape
    D = xall.shape[1]
    C = T // 2
    SLAB = 2 * T
    NC = 4
    KT = 256 if SLAB % 256 == 0 else C
    c = lax.axis_index("ctx")
    h = lax.axis_index("head")
    x = c % 2
    ox = 1 - x
    zz = c // 2
    sh = h + 1 - 2 * (h % 2)
    yh = (h + 2) % 4
    me = (c, h)
    sib = (c, sh)
    yn = (c, yh)
    xc = c + 1 - 2 * x
    xn = (xc, h)
    prv = (c - 2, h)
    nxt = (c + 2, h)
    hasp = zz > 0
    hasn = zz < line - 1
    peers = [(c if dx == 0 else xc, (h + dh) % 4, dx, dh) for dx in (0, 1) for dh in range(4) if dx + dh > 0]

    def rc(src, dst, ssem, rsem, dev):
        return pltpu.make_async_remote_copy(
            src_ref=src, dst_ref=dst, send_sem=ssem, recv_sem=rsem, device_id=dev, device_id_type=MESH
        )

    bar = pltpu.get_barrier_semaphore()
    for pc, ph, _, _ in peers:
        pl.semaphore_signal(bar, inc=1, device_id=(pc, ph), device_id_type=MESH)

    @pl.when(hasp)
    def _():
        pl.semaphore_signal(bar, inc=1, device_id=prv, device_id_type=MESH)

    @pl.when(hasn)
    def _():
        pl.semaphore_signal(bar, inc=1, device_id=nxt, device_id_type=MESH)

    pl.semaphore_wait(bar, 7 + hasp.astype(jnp.int32) + hasn.astype(jnp.int32))

    def al(v, m):
        return pl.multiple_of(v, m)

    def piece(g, r, hh):
        return xall.at[pl.ds(al(g * T + r * C, C), C), pl.ds(al(hh * F, F), F)]

    def own_copy(r, slot, kind, dev):
        return rc(ev.at[pl.ds(r * C, C)], piece(x, r, h), sA.at[slot, r], rA.at[kind, r], dev)

    def relay(g, r, hh, slot, kind, dev):
        p = piece(g, r, hh)
        return rc(p, p, sA.at[slot, r], rA.at[kind, r], dev)

    def got(g, r, hh, kind):
        p = piece(g, r, hh)
        rc(p, p, sA.at[0, r], rA.at[kind, r], sib).wait_recv()

    sendsA = []

    def go_send(d):
        d.start()
        sendsA.append(d)

    for r in (0, 1):
        go_send(own_copy(r, 1, 4, yn))
        go_send(own_copy(r, 2, 5, xn))
        go_send(own_copy(r, 0, 0, sib))
    xall[pl.ds(al(x * T, T), T), pl.ds(al(h * F, F), F)] = ev[...]

    def chunk_base(i):
        r = i % 2
        g = jnp.where(i < 2, x, ox)
        return al(g * T + r * C, C)

    RB = 128 if C % 128 == 0 else C
    LN = 64 if C % 64 == 0 else C

    def qcopy(s, i, dev):
        rows = pl.ds(chunk_base(i), C)
        return rc(qbuf.at[s, rows], qbuf.at[s, rows], qs.at[s, i], qr.at[s, i], dev)

    def kcopy(i):
        cols = pl.ds(chunk_base(i), C)
        return rc(kbuf.at[:, cols], kprev.at[:, cols], ks.at[i], kr.at[i], nxt)

    def vcopy(i):
        rows = pl.ds(chunk_base(i), C)
        return rc(vbuf.at[rows], vprev.at[rows], vs.at[i], vr.at[i], nxt)

    def project(i):
        base = chunk_base(i)

        def ln(k, carry):
            rows = pl.ds(al(base + k * LN, LN), LN)
            xf = xall[rows, :].astype(F32)
            mean = jnp.mean(xf, axis=-1, keepdims=True)
            cen = xf - mean
            var = jnp.mean(cen * cen, axis=-1, keepdims=True)
            nbuf[pl.ds(al(k * LN, LN), LN), :] = (cen * lax.rsqrt(var + EPS) * gain[...]).astype(BF16)
            return carry

        lax.fori_loop(0, C // LN, ln, 0)
        rows = pl.ds(base, C)
        for half in (1, 0):
            p = silu(
                jnp.dot(nbuf[...], w[:, half * 2 * HDIM:(half + 1) * 2 * HDIM], preferred_element_type=F32)
            ).astype(BF16)
            if half == 1:
                qbuf[zz, rows, :] = p[:, :HDIM]
                kbuf[:, rows] = p[:, HDIM:].astype(F32).T.astype(BF16)

                @pl.when(zz > 1)
                def _():
                    qcopy(zz, i, prv).start()

                @pl.when(hasn)
                def _():
                    kcopy(i).start()
            else:
                gate[rows, :] = p[:, :HDIM]
                vbuf[rows, :] = p[:, HDIM:]

                @pl.when(hasn)
                def _():
                    vcopy(i).start()

    h3 = sh + 2 - 4 * (sh // 2)
    got(x, 0, yh, 4)
    go_send(relay(x, 0, yh, 3, 1, sib))
    got(ox, 0, h, 5)
    go_send(relay(ox, 0, h, 6, 6, yn))
    go_send(relay(ox, 0, h, 4, 2, sib))
    got(x, 0, sh, 0)
    got(x, 0, h3, 1)
    project(0)
    got(x, 1, yh, 4)
    go_send(relay(x, 1, yh, 6, 6, xn))
    go_send(relay(x, 1, yh, 3, 1, sib))
    got(ox, 1, h, 5)
    go_send(relay(ox, 1, h, 4, 2, sib))
    got(x, 1, sh, 0)
    got(x, 1, h3, 1)
    project(1)
    for r in (0, 1):
        got(ox, r, yh, 6)
        go_send(relay(ox, r, yh, 5, 3, sib))
    for dh in (1, 2, 3):
        ph = (h + dh) % 4
        go_send(
            rc(wout.at[:, pl.ds(al(ph * F, F), F)], wall.at[pl.ds(al(h * F, F), F)],
               ws.at[dh - 1], wr.at[dh - 1], (c, ph))
        )
    wall[pl.ds(al(h * F, F), F), :] = wout[:, pl.ds(al(h * F, F), F)]
    for r in (0, 1):
        got(ox, r, sh, 2)
        got(ox, r, h3, 3)
        project(2 + r)

    half_scale = 0.5 * HDIM ** (-0.5)

    def starts_of(first):
        pos = first + lax.broadcasted_iota(jnp.int32, (C, 1), 0)
        end = jnp.int32(0)
        start = jnp.zeros((C, 1), jnp.int32)
        for s in range(lengths.shape[0]):
            end = end + lengths[s]
            start = jnp.where(pos >= end, end, start)
        return pos, start

    def tile_weights(q, start, pos, k0, keys, first):
        t = jnp.dot(q, keys[:, pl.ds(k0, KT)], preferred_element_type=F32) * half_scale
        wgt = t + t * jnp.tanh(t)
        kpos = first + k0 + lax.broadcasted_iota(jnp.int32, (1, KT), 1)
        allowed = kpos >= start
        if pos is not None:
            allowed = allowed & (kpos <= pos)
        return jnp.where(allowed, wgt, 0.0).astype(BF16)

    def whole_slab(q, start, keys, values, first):
        parts = []
        for b in range(C // RB):
            blk = slice(b * RB, (b + 1) * RB)
            for k in range(SLAB // KT):
                wgt_buf[blk, k * KT:(k + 1) * KT] = tile_weights(q[blk], start[blk], None, k * KT, keys, first)
            parts.append(jnp.dot(wgt_buf[blk, :], values[...], preferred_element_type=F32))
        return jnp.concatenate(parts, axis=0)

    def diagonal(i, carry):
        base = chunk_base(i)
        rows = pl.ds(base, C)
        q = qbuf[zz, rows, :]
        pos, start = starts_of(zz * SLAB + base)
        att[rows, :] = jnp.zeros((C, HDIM), F32)

        def one(k, carry):
            k0 = al(k * KT, KT)
            wgt = tile_weights(q, start, pos, k0, kbuf, zz * SLAB)
            att[rows, :] += jnp.dot(wgt, vbuf[pl.ds(k0, KT), :], preferred_element_type=F32)
            return carry

        lax.fori_loop(0, (base + C + KT - 1) // KT, one, 0)
        return carry

    @pl.when(zz == 0)
    def _():
        lax.fori_loop(0, NC, diagonal, 0)

    def rcopy(s, i, dev):
        rows = pl.ds(chunk_base(i), C)
        return rc(res_out.at[s, rows], res_in.at[s, rows], rs.at[s, i], rr.at[s, i], dev)

    def passing(i, carry):
        qcopy(zz + 1, i, prv).wait_recv()
        qcopy(zz + 1, i, prv).start()
        return carry

    @pl.when(hasp & hasn)
    def _():
        lax.fori_loop(0, NC, passing, 0)

    def pass_on(s, i):
        rows = pl.ds(chunk_base(i), C)
        return rc(res_in.at[s, rows], res_in.at[s, rows], rs.at[s, i], rr.at[s, i], nxt)

    def straight(i, carry):
        rcopy(zz + 1, i, nxt).wait_recv()
        pass_on(zz + 1, i).start()
        return carry

    def onward(t, carry):
        s = zz + 2 + t // NC
        i = t % NC
        rows = pl.ds(chunk_base(i), C)
        rcopy(s, i, nxt).wait_recv()
        res_out[s, rows, :] = (resf[s, rows, :] + res_in[s, rows, :].astype(F32)).astype(BF16)
        rcopy(s, i, nxt).start()
        return carry

    items = jnp.where(zz < line - 2, NC * (line - 2 - zz), 0)
    early = (zz == 1) & (items > 0)

    def incoming(t, carry):
        s = zz + 2 + t // NC
        i = t % NC
        base = chunk_base(i)
        qcopy(s, i, prv).wait_recv()

        @pl.when(hasp)
        def _():
            qcopy(s, i, prv).start()

        rows = pl.ds(base, C)
        q = qbuf[s, rows, :]
        _, start = starts_of(s * SLAB + base)
        total = whole_slab(q, start, kbuf, vbuf, zz * SLAB)

        @pl.when(hasp)
        def _():
            resf[s, rows, :] = total

        @pl.when(zz == 0)
        def _():
            res_out[s, rows, :] = total.astype(BF16)
            rcopy(s, i, nxt).start()

        @pl.when(early & (t < NC))
        def _():
            straight(i, 0)

        return carry

    lax.fori_loop(0, items, incoming, 0)

    @pl.when(hasp)
    def _():
        lax.fori_loop(0, NC, diagonal, 0)

        for i in range(NC):
            kcopy(i).wait_recv()
            vcopy(i).wait_recv()

        @pl.when(items > 0)
        def _():
            onward(0, 0)

        def crossing(i, carry):
            @pl.when((items > 0) & (i < NC - 1))
            def _():
                onward(i + 1, 0)

            base = chunk_base(i)
            rows = pl.ds(base, C)
            _, start = starts_of(zz * SLAB + base)
            att[rows, :] += whole_slab(qbuf[zz, rows, :], start, kprev, vprev, (zz - 1) * SLAB)
            return carry

        lax.fori_loop(0, NC, crossing, 0)

    @pl.when(hasp & hasn & jnp.logical_not(early))
    def _():
        lax.fori_loop(0, NC, straight, 0)

    @pl.when(hasp)
    def _():
        lax.fori_loop(NC, jnp.maximum(items, NC), onward, 0)

    def epiece(xs, r, hs):
        return go.at[pl.ds(r * C, C), pl.ds(al(hs * F + xs * HDIM, HDIM), HDIM)]

    def erelay(xs, r, hs, slot, kind, dev):
        p = epiece(xs, r, hs)
        return rc(p, p, sE.at[slot, r], rE.at[kind, r], dev)

    def egot(xs, r, hs, kind):
        p = epiece(xs, r, hs)
        rc(p, p, sE.at[0, r], rE.at[kind, r], sib).wait_recv()

    ones = jnp.ones((8, HDIM), BF16)
    for i in range(NC):
        r = i % 2
        base = chunk_base(jnp.int32(i))
        rows = pl.ds(base, C)

        @pl.when(zz > 1)
        def _():
            rcopy(zz, i, nxt).wait_recv()
            att[rows, :] += res_in[zz, rows, :].astype(F32)

        a = att[rows, :]
        gs[rows, :] = (a * gate[rows, :].astype(F32)).astype(BF16)
        src = gs.at[rows]
        if i < 2:
            go_send(rc(src, epiece(x, r, h), sE.at[1, r], rE.at[4, r], yn))
            go_send(rc(src, epiece(x, r, h), sE.at[0, r], rE.at[0, r], sib))
            go[r * C:(r + 1) * C, pl.ds(al(h * F + x * HDIM, HDIM), HDIM)] = gs[rows, :]
        else:
            go_send(rc(src, epiece(x, r, h), sE.at[2, r], rE.at[5, r], xn))
        sq = a * a
        hi = sq.astype(BF16)
        lo = (sq - hi.astype(F32)).astype(BF16)
        dims = (((1,), (1,)), ((), ()))
        sqs[:, pl.ds(base, C)] = lax.dot_general(ones, hi, dims, preferred_element_type=F32) + lax.dot_general(
            ones, lo, dims, preferred_element_type=F32
        )
    for n, (pc, ph, dx, dh) in enumerate(peers):
        grp = x if dx == 0 else ox
        go_send(rc(sqs.at[:, pl.ds(al(grp * T, T), T)], sqall.at[n], ss.at[n], sr.at[n], (pc, ph)))
    for r in (0, 1):
        egot(x, r, yh, 4)
        go_send(erelay(x, r, yh, 3, 1, sib))
    for r in (0, 1):
        egot(ox, r, h, 5)
        go_send(erelay(ox, r, h, 6, 6, yn))
        go_send(erelay(ox, r, h, 4, 2, sib))
    for dh in (1, 2, 3):
        src_h = (h + 4 - dh) % 4
        rc(wout.at[:, pl.ds(0, F)], wall.at[pl.ds(al(src_h * F, F), F)], ws.at[dh - 1], wr.at[dh - 1], sib).wait_recv()
    squares = sqs[:, pl.ds(al(x * T, T), T)]
    for n in range(7):
        rc(sqs.at[:, pl.ds(0, T)], sqall.at[n], ss.at[n], sr.at[n], sib).wait_recv()
        squares = squares + sqall[n]
    inv = lax.rsqrt(squares / D + EPS)
    inv = jnp.broadcast_to(inv[0:1], (HDIM, T)).T
    for r in (0, 1):
        egot(ox, r, yh, 6)
        go_send(erelay(ox, r, yh, 5, 3, sib))
    for r in (0, 1):
        egot(x, r, sh, 0)
        egot(x, r, h3, 1)
        egot(ox, r, sh, 2)
        egot(ox, r, h3, 3)
        rows = slice(r * C, (r + 1) * C)
        prod = jnp.dot(go[rows, :], wall[...], preferred_element_type=F32)
        scale = inv[rows, :]
        for k in range(F // HDIM):
            cols = slice(k * HDIM, (k + 1) * HDIM)
            out[rows, cols] = (ev[rows, cols].astype(F32) + prod[:, cols] * scale).astype(BF16)

    for d in sendsA:
        d.wait_send()

    @pl.when(hasn)
    def _():
        for i in range(NC):
            kcopy(i).wait_send()
            vcopy(i).wait_send()

    @pl.when(zz > 1)
    def _():
        for i in range(NC):
            qcopy(zz, i, prv).wait_send()

    @pl.when(hasp & hasn)
    def _():
        def fin(t, carry):
            qcopy(zz + 1 + t // NC, t % NC, prv).wait_send()
            rcopy(zz + 1 + t // NC, t % NC, nxt).wait_send()
            return carry

        lax.fori_loop(0, items + NC, fin, 0)

    @pl.when(zz == 0)
    def _():
        def fin(t, carry):
            rcopy(2 + t // NC, t % NC, nxt).wait_send()
            return carry

        lax.fori_loop(0, items, fin, 0)


def shards(events, norm_gain, w_uvqk, w_out, lengths):
    T, F = events.shape
    D = w_uvqk.shape[0]
    line = lax.axis_size("ctx") // 2
    x = lax.axis_index("ctx") % 2
    w = lax.dynamic_slice_in_dim(w_uvqk, x * HDIM, HDIM, 2).reshape(D, 4 * HDIM)
    S = 2 * T
    vm = pltpu.VMEM
    dma = pltpu.SemaphoreType.DMA
    vspec = pl.BlockSpec(memory_space=pltpu.VMEM)
    return pl.pallas_call(
        functools.partial(kernel, line),
        out_shape=jax.ShapeDtypeStruct((T, F), BF16),
        in_specs=[vspec] * 4 + [pl.BlockSpec(memory_space=pltpu.SMEM)],
        out_specs=vspec,
        scratch_shapes=[
            vm((S, D), BF16), vm((T // 2, D), BF16), vm((HDIM, S), BF16), vm((T // 2, S), BF16), vm((S, HDIM), BF16),
            vm((HDIM, S), BF16), vm((S, HDIM), BF16),
            vm((S, HDIM), BF16),
            vm((line, S, HDIM), BF16), vm((line, S, HDIM), F32), vm((line, S, HDIM), BF16),
            vm((line, S, HDIM), BF16), vm((S, HDIM), F32), vm((S, HDIM), BF16), vm((T, D), BF16),
            vm((8, S), F32), vm((7, 8, T), F32), vm((D, F), BF16),
            dma((7, 2)), dma((7, 2)), dma((line, 4)), dma((line, 4)), dma((line, 4)), dma((line, 4)),
            dma((7, 2)), dma((7, 2)), dma((3,)), dma((3,)), dma((7,)), dma((7,)),
            dma((4,)), dma((4,)), dma((4,)), dma((4,)),
        ],
        compiler_params=pltpu.CompilerParams(
            collective_id=0, has_side_effects=True, vmem_limit_bytes=56 * 1024 * 1024
        ),
    )(events, norm_gain.reshape(1, D), w, w_out, lengths)


def solution(mesh):
    in_specs = (P("ctx", "head"), P(), P(None, None, "head"), P("head", None), P())
    return jax.shard_map(shards, mesh=mesh, in_specs=in_specs, out_specs=P("ctx", "head"), check_vma=False)
```

```python
import functools

import jax
import jax.numpy as jnp
from jax import lax
from jax.experimental import pallas as pl
from jax.experimental.pallas import tpu as pltpu
from jax.sharding import PartitionSpec as P

HDIM = 128
EPS = 1e-05
MESH = pl.DeviceIdType.MESH
F32 = jnp.float32
BF16 = jnp.bfloat16


def silu(z):
    t = 0.5 * z
    return t + t * jnp.tanh(t)


def kernel(
    line, ev, gain, w, wout, lengths, out,
    xall, nbuf, kbuf, wgt_buf, vbuf, kprev, vprev, gate, qbuf, resf, res_in, res_out, att, gs, go, sqs, sqall, wall,
    sA, rA, qs, qr, rs, rr, sE, rE, ws, wr, ss, sr, ks, kr, vs, vr,
):
    T, F = ev.shape
    D = xall.shape[1]
    C = T // 2
    SLAB = 2 * T
    NC = 4
    KT = 256 if SLAB % 256 == 0 else C
    c = lax.axis_index("ctx")
    h = lax.axis_index("head")
    x = c % 2
    ox = 1 - x
    zz = c // 2
    sh = h + 1 - 2 * (h % 2)
    yh = (h + 2) % 4
    me = (c, h)
    sib = (c, sh)
    yn = (c, yh)
    xc = c + 1 - 2 * x
    xn = (xc, h)
    prv = (c - 2, h)
    nxt = (c + 2, h)
    hasp = zz > 0
    hasn = zz < line - 1
    peers = [(c if dx == 0 else xc, (h + dh) % 4, dx, dh) for dx in (0, 1) for dh in range(4) if dx + dh > 0]

    def rc(src, dst, ssem, rsem, dev):
        return pltpu.make_async_remote_copy(
            src_ref=src, dst_ref=dst, send_sem=ssem, recv_sem=rsem, device_id=dev, device_id_type=MESH
        )

    bar = pltpu.get_barrier_semaphore()
    for pc, ph, _, _ in peers:
        pl.semaphore_signal(bar, inc=1, device_id=(pc, ph), device_id_type=MESH)

    @pl.when(hasp)
    def _():
        pl.semaphore_signal(bar, inc=1, device_id=prv, device_id_type=MESH)

    @pl.when(hasn)
    def _():
        pl.semaphore_signal(bar, inc=1, device_id=nxt, device_id_type=MESH)

    pl.semaphore_wait(bar, 7 + hasp.astype(jnp.int32) + hasn.astype(jnp.int32))

    def al(v, m):
        return pl.multiple_of(v, m)

    def piece(g, r, hh):
        return xall.at[pl.ds(al(g * T + r * C, C), C), pl.ds(al(hh * F, F), F)]

    def own_copy(r, slot, kind, dev):
        return rc(ev.at[pl.ds(r * C, C)], piece(x, r, h), sA.at[slot, r], rA.at[kind, r], dev)

    def relay(g, r, hh, slot, kind, dev):
        p = piece(g, r, hh)
        return rc(p, p, sA.at[slot, r], rA.at[kind, r], dev)

    def got(g, r, hh, kind):
        p = piece(g, r, hh)
        rc(p, p, sA.at[0, r], rA.at[kind, r], sib).wait_recv()

    sendsA = []

    def go_send(d):
        d.start()
        sendsA.append(d)

    for r in (0, 1):
        go_send(own_copy(r, 1, 4, yn))
        go_send(own_copy(r, 2, 5, xn))
        go_send(own_copy(r, 0, 0, sib))
    xall[pl.ds(al(x * T, T), T), pl.ds(al(h * F, F), F)] = ev[...]

    def chunk_base(i):
        r = i % 2
        g = jnp.where(i < 2, x, ox)
        return al(g * T + r * C, C)

    RB = 128 if C % 128 == 0 else C
    LN = 64 if C % 64 == 0 else C

    def qcopy(s, i, dev):
        rows = pl.ds(chunk_base(i), C)
        return rc(qbuf.at[s, rows], qbuf.at[s, rows], qs.at[s, i], qr.at[s, i], dev)

    def kcopy(i):
        cols = pl.ds(chunk_base(i), C)
        return rc(kbuf.at[:, cols], kprev.at[:, cols], ks.at[i], kr.at[i], nxt)

    def vcopy(i):
        rows = pl.ds(chunk_base(i), C)
        return rc(vbuf.at[rows], vprev.at[rows], vs.at[i], vr.at[i], nxt)

    half_scale = 0.5 * HDIM ** (-0.5)

    def project(i):
        base = chunk_base(i)

        def ln(k, carry):
            rows = pl.ds(al(base + k * LN, LN), LN)
            xf = xall[rows, :].astype(F32)
            mean = jnp.mean(xf, axis=-1, keepdims=True)
            cen = xf - mean
            var = jnp.mean(cen * cen, axis=-1, keepdims=True)
            nbuf[pl.ds(al(k * LN, LN), LN), :] = (cen * lax.rsqrt(var + EPS) * gain[...]).astype(BF16)
            return carry

        lax.fori_loop(0, C // LN, ln, 0)
        rows = pl.ds(base, C)
        for half in (1, 0):
            p = silu(
                jnp.dot(nbuf[...], w[:, half * 2 * HDIM:(half + 1) * 2 * HDIM], preferred_element_type=F32)
            )
            if half == 1:
                qbuf[zz, rows, :] = (p[:, :HDIM] * half_scale).astype(BF16)
                kbuf[:, rows] = p[:, HDIM:].T.astype(BF16)

                @pl.when(zz > 1)
                def _():
                    qcopy(zz, i, prv).start()

                @pl.when(hasn)
                def _():
                    kcopy(i).start()
            else:
                gate[rows, :] = p[:, :HDIM].astype(BF16)
                vbuf[rows, :] = p[:, HDIM:].astype(BF16)

                @pl.when(hasn)
                def _():
                    vcopy(i).start()

    h3 = sh + 2 - 4 * (sh // 2)
    got(x, 0, yh, 4)
    go_send(relay(x, 0, yh, 3, 1, sib))
    got(ox, 0, h, 5)
    go_send(relay(ox, 0, h, 6, 6, yn))
    go_send(relay(ox, 0, h, 4, 2, sib))
    got(x, 0, sh, 0)
    got(x, 0, h3, 1)
    project(0)
    got(x, 1, yh, 4)
    go_send(relay(x, 1, yh, 6, 6, xn))
    go_send(relay(x, 1, yh, 3, 1, sib))
    got(ox, 1, h, 5)
    go_send(relay(ox, 1, h, 4, 2, sib))
    got(x, 1, sh, 0)
    got(x, 1, h3, 1)
    project(1)
    for r in (0, 1):
        got(ox, r, yh, 6)
        go_send(relay(ox, r, yh, 5, 3, sib))
    for dh in (1, 2, 3):
        ph = (h + dh) % 4
        go_send(
            rc(wout.at[:, pl.ds(al(ph * F, F), F)], wall.at[pl.ds(al(h * F, F), F)],
               ws.at[dh - 1], wr.at[dh - 1], (c, ph))
        )
    wall[pl.ds(al(h * F, F), F), :] = wout[:, pl.ds(al(h * F, F), F)]
    for r in (0, 1):
        got(ox, r, sh, 2)
        got(ox, r, h3, 3)
        project(2 + r)

    def starts_of(first):
        pos = first + lax.broadcasted_iota(jnp.int32, (C, 1), 0)
        end = jnp.int32(0)
        start = jnp.zeros((C, 1), jnp.int32)
        for s in range(lengths.shape[0]):
            end = end + lengths[s]
            start = jnp.where(pos >= end, end, start)
        return pos, start

    def tile_weights(q, start, pos, k0, keys, first):
        t = jnp.dot(q, keys[:, pl.ds(k0, KT)], preferred_element_type=F32)
        wgt = t + t * jnp.tanh(t)
        kpos = first + k0 + lax.broadcasted_iota(jnp.int32, (1, KT), 1)
        allowed = kpos >= start
        if pos is not None:
            allowed = allowed & (kpos <= pos)
        return jnp.where(allowed, wgt, 0.0).astype(BF16)

    def whole_slab(q, start, keys, values, first):
        parts = []
        for b in range(C // RB):
            blk = slice(b * RB, (b + 1) * RB)
            for k in range(SLAB // KT):
                wgt_buf[blk, k * KT:(k + 1) * KT] = tile_weights(q[blk], start[blk], None, k * KT, keys, first)
            parts.append(jnp.dot(wgt_buf[blk, :], values[...], preferred_element_type=F32))
        return jnp.concatenate(parts, axis=0)

    def diagonal(i, carry):
        base = chunk_base(i)
        rows = pl.ds(base, C)
        q = qbuf[zz, rows, :]
        pos, start = starts_of(zz * SLAB + base)
        att[rows, :] = jnp.zeros((C, HDIM), F32)

        def one(k, carry):
            k0 = al(k * KT, KT)
            wgt = tile_weights(q, start, pos, k0, kbuf, zz * SLAB)
            att[rows, :] += jnp.dot(wgt, vbuf[pl.ds(k0, KT), :], preferred_element_type=F32)
            return carry

        lax.fori_loop(0, (base + C + KT - 1) // KT, one, 0)
        return carry

    @pl.when(zz == 0)
    def _():
        lax.fori_loop(0, NC, diagonal, 0)

    def rcopy(s, i, dev):
        rows = pl.ds(chunk_base(i), C)
        return rc(res_out.at[s, rows], res_in.at[s, rows], rs.at[s, i], rr.at[s, i], dev)

    def passing(i, carry):
        qcopy(zz + 1, i, prv).wait_recv()
        qcopy(zz + 1, i, prv).start()
        return carry

    @pl.when(hasp & hasn)
    def _():
        lax.fori_loop(0, NC, passing, 0)

    def pass_on(s, i):
        rows = pl.ds(chunk_base(i), C)
        return rc(res_in.at[s, rows], res_in.at[s, rows], rs.at[s, i], rr.at[s, i], nxt)

    def straight(i, carry):
        rcopy(zz + 1, i, nxt).wait_recv()
        pass_on(zz + 1, i).start()
        return carry

    def onward(t, carry):
        s = zz + 2 + t // NC
        i = t % NC
        rows = pl.ds(chunk_base(i), C)
        rcopy(s, i, nxt).wait_recv()
        res_out[s, rows, :] = (resf[s, rows, :] + res_in[s, rows, :].astype(F32)).astype(BF16)
        rcopy(s, i, nxt).start()
        return carry

    items = jnp.where(zz < line - 2, NC * (line - 2 - zz), 0)
    early = (zz == 1) & (items > 0)

    def incoming(t, carry):
        s = zz + 2 + t // NC
        i = t % NC
        base = chunk_base(i)
        qcopy(s, i, prv).wait_recv()

        @pl.when(hasp)
        def _():
            qcopy(s, i, prv).start()

        rows = pl.ds(base, C)
        q = qbuf[s, rows, :]
        _, start = starts_of(s * SLAB + base)
        total = whole_slab(q, start, kbuf, vbuf, zz * SLAB)

        @pl.when(hasp)
        def _():
            resf[s, rows, :] = total

        @pl.when(zz == 0)
        def _():
            res_out[s, rows, :] = total.astype(BF16)
            rcopy(s, i, nxt).start()

        @pl.when(early & (t < NC))
        def _():
            straight(i, 0)

        return carry

    lax.fori_loop(0, items, incoming, 0)

    @pl.when(hasp)
    def _():
        lax.fori_loop(0, NC, diagonal, 0)

        for i in range(NC):
            kcopy(i).wait_recv()
            vcopy(i).wait_recv()

        @pl.when(items > 0)
        def _():
            onward(0, 0)

        def crossing(i, carry):
            @pl.when((items > 0) & (i < NC - 1))
            def _():
                onward(i + 1, 0)

            base = chunk_base(i)
            rows = pl.ds(base, C)
            _, start = starts_of(zz * SLAB + base)
            att[rows, :] += whole_slab(qbuf[zz, rows, :], start, kprev, vprev, (zz - 1) * SLAB)
            return carry

        lax.fori_loop(0, NC, crossing, 0)

    @pl.when(hasp & hasn & jnp.logical_not(early))
    def _():
        lax.fori_loop(0, NC, straight, 0)

    @pl.when(hasp)
    def _():
        lax.fori_loop(NC, jnp.maximum(items, NC), onward, 0)

    def epiece(xs, r, hs):
        return go.at[pl.ds(r * C, C), pl.ds(al(hs * F + xs * HDIM, HDIM), HDIM)]

    def erelay(xs, r, hs, slot, kind, dev):
        p = epiece(xs, r, hs)
        return rc(p, p, sE.at[slot, r], rE.at[kind, r], dev)

    def egot(xs, r, hs, kind):
        p = epiece(xs, r, hs)
        rc(p, p, sE.at[0, r], rE.at[kind, r], sib).wait_recv()

    ones = jnp.ones((8, HDIM), BF16)
    for i in range(NC):
        r = i % 2
        base = chunk_base(jnp.int32(i))
        rows = pl.ds(base, C)

        @pl.when(zz > 1)
        def _():
            rcopy(zz, i, nxt).wait_recv()
            att[rows, :] += res_in[zz, rows, :].astype(F32)

        a = att[rows, :]
        gs[rows, :] = (a * gate[rows, :].astype(F32)).astype(BF16)
        src = gs.at[rows]
        if i < 2:
            go_send(rc(src, epiece(x, r, h), sE.at[1, r], rE.at[4, r], yn))
            go_send(rc(src, epiece(x, r, h), sE.at[0, r], rE.at[0, r], sib))
            go[r * C:(r + 1) * C, pl.ds(al(h * F + x * HDIM, HDIM), HDIM)] = gs[rows, :]
        else:
            go_send(rc(src, epiece(x, r, h), sE.at[2, r], rE.at[5, r], xn))
        sq = a * a
        hi = sq.astype(BF16)
        lo = (sq - hi.astype(F32)).astype(BF16)
        dims = (((1,), (1,)), ((), ()))
        sqs[:, pl.ds(base, C)] = lax.dot_general(ones, hi, dims, preferred_element_type=F32) + lax.dot_general(
            ones, lo, dims, preferred_element_type=F32
        )
    for n, (pc, ph, dx, dh) in enumerate(peers):
        grp = x if dx == 0 else ox
        go_send(rc(sqs.at[:, pl.ds(al(grp * T, T), T)], sqall.at[n], ss.at[n], sr.at[n], (pc, ph)))
    for r in (0, 1):
        egot(x, r, yh, 4)
        go_send(erelay(x, r, yh, 3, 1, sib))
    for r in (0, 1):
        egot(ox, r, h, 5)
        go_send(erelay(ox, r, h, 6, 6, yn))
        go_send(erelay(ox, r, h, 4, 2, sib))
    for dh in (1, 2, 3):
        src_h = (h + 4 - dh) % 4
        rc(wout.at[:, pl.ds(0, F)], wall.at[pl.ds(al(src_h * F, F), F)], ws.at[dh - 1], wr.at[dh - 1], sib).wait_recv()
    squares = sqs[:, pl.ds(al(x * T, T), T)]
    for n in range(7):
        rc(sqs.at[:, pl.ds(0, T)], sqall.at[n], ss.at[n], sr.at[n], sib).wait_recv()
        squares = squares + sqall[n]
    inv = lax.rsqrt(squares / D + EPS)
    inv = jnp.broadcast_to(inv[0:1], (HDIM, T)).T
    for r in (0, 1):
        egot(ox, r, yh, 6)
        go_send(erelay(ox, r, yh, 5, 3, sib))
    for r in (0, 1):
        egot(x, r, sh, 0)
        egot(x, r, h3, 1)
        egot(ox, r, sh, 2)
        egot(ox, r, h3, 3)
        rows = slice(r * C, (r + 1) * C)
        prod = jnp.dot(go[rows, :], wall[...], preferred_element_type=F32)
        scale = inv[rows, :]
        for k in range(F // HDIM):
            cols = slice(k * HDIM, (k + 1) * HDIM)
            out[rows, cols] = (ev[rows, cols].astype(F32) + prod[:, cols] * scale).astype(BF16)

    for d in sendsA:
        d.wait_send()

    @pl.when(hasn)
    def _():
        for i in range(NC):
            kcopy(i).wait_send()
            vcopy(i).wait_send()

    @pl.when(zz > 1)
    def _():
        for i in range(NC):
            qcopy(zz, i, prv).wait_send()

    @pl.when(hasp & hasn)
    def _():
        def fin(t, carry):
            qcopy(zz + 1 + t // NC, t % NC, prv).wait_send()
            rcopy(zz + 1 + t // NC, t % NC, nxt).wait_send()
            return carry

        lax.fori_loop(0, items + NC, fin, 0)

    @pl.when(zz == 0)
    def _():
        def fin(t, carry):
            rcopy(2 + t // NC, t % NC, nxt).wait_send()
            return carry

        lax.fori_loop(0, items, fin, 0)


def shards(events, norm_gain, w_uvqk, w_out, lengths):
    T, F = events.shape
    D = w_uvqk.shape[0]
    line = lax.axis_size("ctx") // 2
    x = lax.axis_index("ctx") % 2
    w = lax.dynamic_slice_in_dim(w_uvqk, x * HDIM, HDIM, 2).reshape(D, 4 * HDIM)
    S = 2 * T
    vm = pltpu.VMEM
    dma = pltpu.SemaphoreType.DMA
    vspec = pl.BlockSpec(memory_space=pltpu.VMEM)
    return pl.pallas_call(
        functools.partial(kernel, line),
        out_shape=jax.ShapeDtypeStruct((T, F), BF16),
        in_specs=[vspec] * 4 + [pl.BlockSpec(memory_space=pltpu.SMEM)],
        out_specs=vspec,
        scratch_shapes=[
            vm((S, D), BF16), vm((T // 2, D), BF16), vm((HDIM, S), BF16), vm((T // 2, S), BF16), vm((S, HDIM), BF16),
            vm((HDIM, S), BF16), vm((S, HDIM), BF16),
            vm((S, HDIM), BF16),
            vm((line, S, HDIM), BF16), vm((line, S, HDIM), F32), vm((line, S, HDIM), BF16),
            vm((line, S, HDIM), BF16), vm((S, HDIM), F32), vm((S, HDIM), BF16), vm((T, D), BF16),
            vm((8, S), F32), vm((7, 8, T), F32), vm((D, F), BF16),
            dma((7, 2)), dma((7, 2)), dma((line, 4)), dma((line, 4)), dma((line, 4)), dma((line, 4)),
            dma((7, 2)), dma((7, 2)), dma((3,)), dma((3,)), dma((7,)), dma((7,)),
            dma((4,)), dma((4,)), dma((4,)), dma((4,)),
        ],
        compiler_params=pltpu.CompilerParams(
            collective_id=0, has_side_effects=True, vmem_limit_bytes=56 * 1024 * 1024
        ),
    )(events, norm_gain.reshape(1, D), w, w_out, lengths)


def solution(mesh):
    in_specs = (P("ctx", "head"), P(), P(None, None, "head"), P("head", None), P())
    return jax.shard_map(shards, mesh=mesh, in_specs=in_specs, out_specs=P("ctx", "head"), check_vma=False)
```
